256 devices in a mesh: dp: 16 (over z_lo, y), tensor: 8 (over x, core), section: 2 (over z_hi).
Axes of the slice: x: 4, y: 4, z: 8 (z_hi: 2, z_lo: 4; z = z_hi * 4 + z_lo), core: 2. Of those that a mesh axis runs over, the one named last changes fastest.
Arguments:
- value_grad: bfloat16 [2, 2048, 12288], P('section', 'dp', 'tensor'), may hold values from -2.5 to 2.5
- value_weight: bfloat16 [2, 12288, 12288], P('section', 'dp', 'tensor'), may hold values from -0.0546875 to 0.0546875
- context: bfloat16 [2, 2048, 12288], P('section', 'dp', 'tensor'), may hold values from -0.1796875 to 0.1796875
- out_weight: bfloat16 [2, 12288, 12288], P('section', 'tensor', 'dp'), may hold values from -0.0546875 to 0.0546875
Outputs:
- out_weight_grad: bfloat16 [2, 12288, 12288], P('section', 'tensor', 'dp')
- context_grad: bfloat16 [2, 2048, 12288], P('section', 'dp', 'tensor')
The draws below stay inside these ranges and needn't reach their ends.
All inputs are finite; a program needn't handle non-finite values.
Results may differ from the reference program's by a relative error of at most 0.023.
Values may be sent and summed in bfloat16 or wider, within the bound.
No kernel may reach another device: no remote copies, remote signals or barrier semaphores. Data moves between devices by JAX's collectives and lax.ppermute only.
A program may use at most 128 MiB of HBM per device.

```python
import jax
import jax.numpy as jnp

D = 12288
TOKENS = 2048
N_DP = 16
N_SECTION = 2


def level_of(key, shape, shards, smallest, largest):
    def one(position, parts):
        heights = jax.random.uniform(jax.random.fold_in(jax.random.fold_in(key, 6), position), (parts,), jnp.float32, smallest / len(shards), largest / len(shards))
        return jnp.repeat(jnp.exp(heights), shape[position] // parts).reshape((-1,) + (1,) * (len(shape) - position - 1))

    level = one(*shards[0])
    for cut in shards[1:]:
        level = level * one(*cut)
    return level


def bell_draw(rng, dims, width, bound, pieces=(), dtype=jnp.bfloat16):
    gain = level_of(rng, dims, pieces, -0.22, 0.18) if pieces else 1.0
    entries = jax.random.normal(rng, dims, jnp.float32) * width * gain
    return jnp.minimum(jnp.maximum(entries, -bound), bound).astype(dtype)


def setup_inputs(seed: int = 0) -> dict:
    keys = jax.random.split(jax.random.key(seed), 5)
    value_grad = bell_draw(keys[0], (N_SECTION, TOKENS, D), 0.4, 2.5, ((0, 2), (1, 16), (2, 8)))
    value_weight = bell_draw(keys[1], (N_SECTION, D, D), D ** -0.5, 0.0546875, ((0, 2), (1, 16), (2, 8)))
    context = bell_draw(keys[2], (N_SECTION, TOKENS, D), 0.03, 0.1796875, ((0, 2), (1, 16), (2, 8)))
    out_weight = bell_draw(keys[3], (N_SECTION, D, D), D ** -0.5, 0.0546875, ((0, 2), (1, 8), (2, 16)))
    return dict(value_grad=value_grad, value_weight=value_weight, context=context, out_weight=out_weight)


def reference(value_grad, value_weight, context, out_weight):
    boundary = []
    for section_index in range(N_SECTION):
        boundary.append(jnp.dot(value_grad[section_index], value_weight[section_index].T, preferred_element_type=jnp.float32).astype(jnp.bfloat16))
    out_grads = []
    context_grads = []
    block = D // N_DP
    for section_index in range(N_SECTION):
        arrived = boundary[1 - section_index]
        out_grads.append(jnp.dot(context[section_index].T, arrived, preferred_element_type=jnp.float32).astype(jnp.bfloat16))
        weight_now = out_weight[section_index]
        total = jnp.zeros((TOKENS, D), jnp.float32)
        for block_index in range(N_DP):
            left = arrived[:, block_index * block:(block_index + 1) * block]
            right = weight_now[:, block_index * block:(block_index + 1) * block]
            part = jnp.dot(left, right.T, preferred_element_type=jnp.float32).astype(jnp.bfloat16)
            total = total + part.astype(jnp.float32)
        context_grads.append(total.astype(jnp.bfloat16))
    return jnp.stack(out_grads), jnp.stack(context_grads)
```

```python
import jax
import jax.numpy as jnp
from jax import lax
from jax.sharding import PartitionSpec as P

F32 = jnp.float32
BF16 = jnp.bfloat16


def dp_move(shard, to):
    pairs = []
    for z in range(4):
        for y in range(4):
            z2, y2 = to(z, y)
            pairs.append((z * 4 + y, z2 % 4 * 4 + y2 % 4))
    return lax.ppermute(shard, "dp", pairs)


def up(z, y):
    return z + 1, y


def down(z, y):
    return z - 1, y


def across(z, y):
    return z + 2, y


def swap(r):
    return lambda z, y: (z, y ^ r)


def tensor_move(shard, dx, dc):
    pairs = [
        (x * 2 + c, (x + dx) % 4 * 2 + (c + dc) % 2) for x in range(4) for c in range(2)
    ]
    return lax.ppermute(shard, "tensor", pairs)


def roll_in(block):
    t = lax.axis_index("tensor")
    x, c = t // 2, t % 2
    rows = block.reshape(4, 2, 16, -1)
    rows = jnp.where(c == 0, rows, rows[:, ::-1])
    twice = jnp.concatenate([rows, rows], 0)
    rows = lax.dynamic_slice_in_dim(twice, x, 4, 0)
    return rows.transpose(1, 0, 2, 3).reshape(128, -1)


def roll_out(block):
    t = lax.axis_index("tensor")
    x, c = t // 2, t % 2
    rows = block.reshape(2, 4, 16, -1).transpose(1, 0, 2, 3)
    twice = jnp.concatenate([rows, rows], 0)
    rows = lax.dynamic_slice_in_dim(twice, (4 - x) % 4, 4, 0)
    rows = jnp.where(c == 0, rows, rows[:, ::-1])
    return rows.reshape(128, -1)


def rows_dot(a, b):
    return lax.dot_general(a, b, (((1,), (1,)), ((), ())), preferred_element_type=F32)


def after(value, *tokens):
    return lax.optimization_barrier((value,) + tokens)[0]


LAG = {"y1": 2, "y3": 2, "z": 1}


class Lanes:
    def __init__(self):
        self.done = {"y1": [], "y3": [], "z": []}

    def send(self, lane, value, to):
        past = self.done[lane]
        lag = LAG[lane]
        if len(past) >= lag:
            value = after(value, past[-lag])
        got = dp_move(value, to)
        past.append(got)
        return got


class Gather:
    def __init__(self, lanes, block, first):
        self.lanes, self.block, self.first = lanes, block, first

    def one(self):
        self.near = self.lanes.send("y%d" % self.first, self.block, swap(self.first))

    def two(self):
        other = 4 - self.first
        both = jnp.concatenate([self.block, self.near], 0)
        got = self.lanes.send("y%d" % other, both, swap(other))
        n = self.block.shape[0]
        found = {0: self.block, self.first: self.near, other: got[:n], 2: got[n:]}
        self.rows = jnp.concatenate([found[r] for r in range(4)], 0)


class Scatter:
    def __init__(self, lanes, parts, first):
        self.lanes, self.parts, self.first = lanes, parts, first

    def one(self):
        first, other = self.first, 4 - self.first
        both = jnp.concatenate([self.parts[first], self.parts[2]], 0)
        got = self.lanes.send("y%d" % first, both, swap(first))
        n = self.parts[0].shape[0]
        self.mine = self.parts[0].astype(F32) + got[:n].astype(F32)
        self.give = (self.parts[other].astype(F32) + got[n:].astype(F32)).astype(BF16)

    def two(self):
        other = 4 - self.first
        got = self.lanes.send("y%d" % other, self.give, swap(other))
        self.total = self.mine + got.astype(F32)


def pair(a, b):
    a.one()
    b.one()
    a.two()
    b.two()


def chain(part):
    n = part.shape[0]
    got = tensor_move(part[:, 1].astype(BF16), 0, 1)
    pair = part[:, 0] + got.astype(F32)
    mine = pair[:, 0]
    for moved in [tensor_move(pair[:, dx].astype(BF16), dx, 0) for dx in (1, 3, 2)]:
        mine = mine + moved.astype(F32)
    arrived = lax.ppermute(mine.astype(BF16), "section", [(0, 1), (1, 0)])
    chunks = [arrived] + [tensor_move(arrived, -dx, 0) for dx in (1, 2, 3)]
    near = jnp.stack(chunks, 1)
    other = tensor_move(near, 0, 1)
    return jnp.stack([near, other], 1).reshape(n * 128, -1)


def body(value_grad, value_weight, context, out_weight):
    w1 = value_weight[0]
    w2 = out_weight[0]
    lanes = Lanes()
    vg = {0: roll_in(value_grad[0])}
    cx = {0: roll_in(context[0])}
    v = {0: Gather(lanes, vg[0], 1)}
    c = {0: Gather(lanes, cx[0], 3)}
    vg[1] = lanes.send("z", vg[0], down)
    vg[2] = lanes.send("z", vg[1], down)
    vg[3] = lanes.send("z", vg[0], up)
    cx[1] = lanes.send("z", cx[0], down)
    cx[2] = lanes.send("z", cx[1], down)
    cx[3] = lanes.send("z", cx[0], up)
    pair(v[0], c[0])
    v[1] = Gather(lanes, vg[1], 3)
    v[2] = Gather(lanes, vg[2], 1)
    pair(v[1], v[2])
    v[3] = Gather(lanes, vg[3], 3)
    c[1] = Gather(lanes, cx[1], 1)
    pair(v[3], c[1])
    c[2] = Gather(lanes, cx[2], 3)
    c[3] = Gather(lanes, cx[3], 1)
    pair(c[2], c[3])
    rows = {}
    totals = {}
    out_grad = 0.0
    for ka, kb in ((1, 2), (3, 0)):
        parts = [rows_dot(v[k].rows, w1).reshape(4, 2, 4, 16, 768) for k in (ka, kb)]
        got = chain(jnp.concatenate(parts, 0))
        cpart = rows_dot(got, w2).astype(BF16).reshape(2, 4, 128, 1536)
        scatters = [Scatter(lanes, [cpart[i, b] for b in range(4)], (1, 3)[i]) for i in range(2)]
        pair(*scatters)
        for i, k in enumerate((ka, kb)):
            total = scatters[i].total
            if k:
                total = dp_move(total.astype(BF16), (None, up, across, down)[k]).astype(F32)
            totals[k] = total
            out_grad = out_grad + lax.dot_general(c[k].rows, got[i * 512 : (i + 1) * 512], (((0,), (0,)), ((), ())), preferred_element_type=F32)
    result = totals[0] + totals[1] + totals[2] + totals[3]
    return out_grad.astype(BF16)[None], roll_out(result.astype(BF16))[None]


def solution(mesh):
    in_specs = (
        P("section", "dp", "tensor"),
        P("section", "dp", "tensor"),
        P("section", "dp", "tensor"),
        P("section", "tensor", "dp"),
    )
    out_specs = (P("section", "tensor", "dp"), P("section", "dp", "tensor"))
    return jax.shard_map(body, mesh=mesh, in_specs=in_specs, out_specs=out_specs, check_vma=False)
```

```python
import jax
import jax.numpy as jnp
from jax import lax
from jax.sharding import PartitionSpec as P

F32 = jnp.float32
BF16 = jnp.bfloat16


def dp_move(shard, to):
    pairs = []
    for z in range(4):
        for y in range(4):
            z2, y2 = to(z, y)
            pairs.append((z * 4 + y, z2 % 4 * 4 + y2 % 4))
    return lax.ppermute(shard, "dp", pairs)


def up(z, y):
    return z + 1, y


def down(z, y):
    return z - 1, y


def across(z, y):
    return z + 2, y


def swap(r):
    return lambda z, y: (z, y ^ r)


def tensor_move(shard, dx, dc):
    pairs = [
        (x * 2 + c, (x + dx) % 4 * 2 + (c + dc) % 2) for x in range(4) for c in range(2)
    ]
    return lax.ppermute(shard, "tensor", pairs)


def roll_in(block):
    t = lax.axis_index("tensor")
    x, c = t // 2, t % 2
    rows = block.reshape(4, 2, 16, -1)
    rows = jnp.where(c == 0, rows, rows[:, ::-1])
    twice = jnp.concatenate([rows, rows], 0)
    rows = lax.dynamic_slice_in_dim(twice, x, 4, 0)
    return rows.transpose(1, 0, 2, 3).reshape(128, -1)


def roll_out(block):
    t = lax.axis_index("tensor")
    x, c = t // 2, t % 2
    rows = block.reshape(2, 4, 16, -1).transpose(1, 0, 2, 3)
    twice = jnp.concatenate([rows, rows], 0)
    rows = lax.dynamic_slice_in_dim(twice, (4 - x) % 4, 4, 0)
    rows = jnp.where(c == 0, rows, rows[:, ::-1])
    return rows.reshape(128, -1)


def rows_dot(a, b):
    return lax.dot_general(a, b, (((1,), (1,)), ((), ())), preferred_element_type=F32)


def after(value, *tokens):
    return lax.optimization_barrier((value,) + tokens)[0]


LAG = {"y1": 99, "y3": 99, "z": 2}


class Lanes:
    def __init__(self):
        self.done = {"y1": [], "y3": [], "z": []}

    def send(self, lane, value, to):
        past = self.done[lane]
        lag = LAG[lane]
        if len(past) >= lag:
            value = after(value, past[-lag])
        got = dp_move(value, to)
        past.append(got)
        return got


class Gather:
    def __init__(self, lanes, block, first):
        self.lanes, self.block, self.first = lanes, block, first

    def one(self):
        self.near = self.lanes.send("y%d" % self.first, self.block, swap(self.first))

    def two(self):
        other = 4 - self.first
        both = jnp.concatenate([self.block, self.near], 0)
        got = self.got = self.lanes.send("y%d" % other, both, swap(other))

    def rows(self, *tokens):
        other = 4 - self.first
        got = after(self.got, *tokens) if tokens else self.got
        n = self.block.shape[0]
        found = {0: self.block, self.first: self.near, other: got[:n], 2: got[n:]}
        return jnp.concatenate([found[r] for r in range(4)], 0)


class Scatter:
    def __init__(self, lanes, parts, first):
        self.lanes, self.parts, self.first = lanes, parts, first

    def one(self):
        first, other = self.first, 4 - self.first
        both = jnp.concatenate([self.parts[first], self.parts[2]], 0)
        got = self.lanes.send("y%d" % first, both, swap(first))
        n = self.parts[0].shape[0]
        self.mine = self.parts[0].astype(F32) + got[:n].astype(F32)
        self.give = (self.parts[other].astype(F32) + got[n:].astype(F32)).astype(BF16)

    def two(self):
        other = 4 - self.first
        got = self.lanes.send("y%d" % other, self.give, swap(other))
        self.total = self.mine + got.astype(F32)


def pair(a, b):
    a.one()
    b.one()
    a.two()
    b.two()


def shares(part, first=(), second=()):
    give = part[:, 1].astype(BF16)
    got = tensor_move(after(give, *first) if first else give, 0, 1)
    pair = part[:, 0] + got.astype(F32)
    if second:
        pair = after(pair, *second)
    mine = pair[:, 0]
    for moved in [tensor_move(pair[:, dx].astype(BF16), dx, 0) for dx in (1, 3, 2)]:
        mine = mine + moved.astype(F32)
    return mine.astype(BF16)


def swap_sections(mine):
    return lax.ppermute(mine, "section", [(0, 1), (1, 0)])


def spread_x(arrived):
    chunks = [arrived] + [tensor_move(arrived, -dx, 0) for dx in (1, 2, 3)]
    return jnp.stack(chunks, 1)


def spread_core(near):
    other = tensor_move(near, 0, 1)
    return jnp.stack([near, other], 1).reshape(near.shape[0] * 128, -1), other


class Halves:
    def __init__(self, kind, lanes, blocks):
        self.kind = kind
        if kind is Gather:
            n = blocks.shape[0] // 2
            self.parts = [Gather(lanes, blocks[:n], 1), Gather(lanes, blocks[n:], 3)]
        else:
            n = blocks[0].shape[0] // 2
            self.parts = [Scatter(lanes, [b[:n] for b in blocks], 1), Scatter(lanes, [b[n:] for b in blocks], 3)]

    def rows(self):
        return self.all

    def run(self):
        self.parts[0].one()
        self.parts[1].one()
        self.two()

    def two(self):
        self.parts[0].two()
        self.parts[1].two()
        if self.kind is Gather:
            low, high = [p.rows().reshape(4, 64, -1) for p in self.parts]
            self.all = jnp.concatenate([low, high], 1).reshape(512, -1)
        else:
            self.total = jnp.concatenate([p.total for p in self.parts], 0)


def fence(*values):
    return lax.optimization_barrier(values)


def cat(*blocks):
    return jnp.concatenate(blocks, 0)


def body(value_grad, value_weight, context, out_weight):
    w1 = value_weight[0]
    w2 = out_weight[0]
    lanes = Lanes()

    def partial(rows):
        return rows_dot(rows, w1).reshape(4, 2, 4, 16, 768)

    def matmul3(got):
        cpart = rows_dot(got, w2).astype(BF16).reshape(2, 4, 128, 1536)
        return [[cpart[i, b] for b in range(4)] for i in range(2)]

    def over_core(part):
        got = tensor_move(part[:, 1].astype(BF16), 0, 1)
        return part[:, 0] + got.astype(F32)

    vg0 = roll_in(value_grad[0])
    v0 = Halves(Gather, lanes, vg0)
    vg1 = lanes.send("z", vg0, down)
    vg2 = lanes.send("z", vg1, down)
    vg3 = lanes.send("z", vg0, up)
    v0.run()
    v1 = Halves(Gather, lanes, vg1)
    v1.run()
    part0 = partial(v0.rows())
    rows1, part0, vg2, vg3, cin = fence(v1.rows(), part0, vg2, vg3, context[0])

    near2 = dp_move(vg2, swap(1))
    near3 = dp_move(vg3, swap(3))
    pair_a = over_core(cat(part0, partial(rows1)))
    c0 = roll_in(cin)
    c1 = dp_move(c0, down)
    near2, near3, pair_a, c0, c1 = fence(near2, near3, pair_a, c0, c1)
    far2 = dp_move(cat(vg2, near2), swap(3))
    far3 = dp_move(cat(vg3, near3), swap(1))
    c2 = dp_move(c1, down)
    shares_a = pair_a[:, 0]
    for dx in (1, 3, 2):
        shares_a = shares_a + tensor_move(pair_a[:, dx].astype(BF16), dx, 0).astype(F32)
    rows = cat(vg2, near2, far2[128:], far2[:128], vg3, far3[:128], far3[128:], near3)
    part_b = rows_dot(rows, w1).reshape(8, 2, 4, 16, 768)
    shares_a, part_b, c0, c1, c2 = fence(shares_a.astype(BF16), part_b, c0, c1, c2)

    near0 = dp_move(c0, swap(1))
    near1 = dp_move(c1, swap(3))
    arrived_a = swap_sections(shares_a)
    pair_b = over_core(part_b)
    near0, near1, arrived_a, pair_b, c0, c1, c2 = fence(near0, near1, arrived_a, pair_b, c0, c1, c2)

    far0 = dp_move(cat(c0, near0), swap(3))
    far1 = dp_move(cat(c1, near1), swap(1))
    shares_b = pair_b[:, 0]
    near = {0: arrived_a}
    for dx in (1, 3, 2):
        moved = tensor_move(jnp.stack([pair_b[:, dx].astype(BF16), arrived_a], 0), dx, 0)
        shares_b = shares_b + moved[0].astype(F32)
        near[4 - dx] = moved[1]
    near_a = jnp.stack([near[d] for d in range(4)], 1)
    far0, far1, c2, shares_b, near_a = fence(far0, far1, c2, shares_b.astype(BF16), near_a)
    ctx = {0: cat(c0, near0, far0[128:], far0[:128]), 1: cat(c1, far1[:128], far1[128:], near1)}

    near2 = dp_move(c2[:64], swap(1))
    near3 = dp_move(c2[64:], swap(3))
    arrived_b = swap_sections(shares_b)
    rows_a, _ = spread_core(near_a)
    blocks_a = matmul3(rows_a)
    near2, near3, arrived_b, rows_a, ctx[0], *flat = fence(near2, near3, arrived_b, rows_a, ctx[0], *blocks_a[0], *blocks_a[1])
    blocks_a = [flat[:4], flat[4:]]

    sa = [Scatter(lanes, blocks_a[i], (1, 3)[i]) for i in range(2)]
    lanes.done = {"y1": [], "y3": [], "z": []}
    sa[0].one()
    sa[1].one()
    rows_b, _ = spread_core(spread_x(arrived_b))
    low = dp_move(ctx[0][:256], up)
    mine0, give0, mine1, give1, near2, near3, rows_b, low, high = fence(sa[0].mine, sa[0].give, sa[1].mine, sa[1].give, near2, near3, rows_b, low, ctx[0][256:])
    sa[0].mine, sa[0].give, sa[1].mine, sa[1].give = mine0, give0, mine1, give1
    blocks_b = matmul3(rows_b)
    high = dp_move(high, up)

    lanes.done = {"y1": [], "y3": [], "z": []}
    sb = [Scatter(lanes, blocks_b[i], (1, 3)[i]) for i in range(2)]
    sb[0].one()
    sb[1].one()
    lanes.done = {"y1": [], "y3": [], "z": []}
    sa[0].two()
    sa[1].two()
    z1 = dp_move(sa[1].total.astype(BF16), up)
    total0, z1, mine2, give2, mine3, give3, near2, near3, low, high = fence(sa[0].total, z1, sb[0].mine, sb[0].give, sb[1].mine, sb[1].give, near2, near3, low, high)
    ctx[3] = cat(low, high)
    sb[0].mine, sb[0].give, sb[1].mine, sb[1].give = mine2, give2, mine3, give3

    lanes.done = {"y1": [], "y3": [], "z": []}
    sb[0].two()
    sb[1].two()
    far2 = dp_move(cat(c2[:64], near2), swap(3))
    far3 = dp_move(cat(c2[64:], near3), swap(1))
    ctx[2] = cat(c2, near2, far3[:64], far2[64:], far3[64:], far2[:64], near3)
    z2 = dp_move(sb[0].total.astype(BF16), across)
    z3 = dp_move(sb[1].total.astype(BF16), down)
    result = total0 + z1.astype(F32) + z2.astype(F32) + z3.astype(F32)

    def grad(k, rows):
        return lax.dot_general(ctx[k], rows, (((0,), (0,)), ((), ())), preferred_element_type=F32)

    out_grad = grad(0, rows_a[:512]) + grad(1, rows_a[512:]) + grad(2, rows_b[:512]) + grad(3, rows_b[512:])
    return out_grad.astype(BF16)[None], roll_out(result.astype(BF16))[None]


def solution(mesh):
    in_specs = (
        P("section", "dp", "tensor"),
        P("section", "dp", "tensor"),
        P("section", "dp", "tensor"),
        P("section", "tensor", "dp"),
    )
    out_specs = (P("section", "tensor", "dp"), P("section", "dp", "tensor"))
    return jax.shard_map(body, mesh=mesh, in_specs=in_specs, out_specs=out_specs, check_vma=False)
```

```python
import jax
import jax.numpy as jnp
from jax import lax
from jax.sharding import PartitionSpec as P

F32 = jnp.float32
BF16 = jnp.bfloat16


def dp_move(shard, to):
    pairs = []
    for z in range(4):
        for y in range(4):
            z2, y2 = to(z, y)
            pairs.append((z * 4 + y, z2 % 4 * 4 + y2 % 4))
    return lax.ppermute(shard, "dp", pairs)


def up(z, y):
    return z + 1, y


def down(z, y):
    return z - 1, y


def across(z, y):
    return z + 2, y


def swap(r):
    return lambda z, y: (z, y ^ r)


def tensor_move(shard, dx, dc):
    pairs = [
        (x * 2 + c, (x + dx) % 4 * 2 + (c + dc) % 2) for x in range(4) for c in range(2)
    ]
    return lax.ppermute(shard, "tensor", pairs)


def roll_in(block):
    t = lax.axis_index("tensor")
    x, c = t // 2, t % 2
    rows = block.reshape(4, 2, 16, -1)
    rows = jnp.where(c == 0, rows, rows[:, ::-1])
    twice = jnp.concatenate([rows, rows], 0)
    rows = lax.dynamic_slice_in_dim(twice, x, 4, 0)
    return rows.transpose(1, 0, 2, 3).reshape(128, -1)


def roll_out(block):
    t = lax.axis_index("tensor")
    x, c = t // 2, t % 2
    rows = block.reshape(2, 4, 16, -1).transpose(1, 0, 2, 3)
    twice = jnp.concatenate([rows, rows], 0)
    rows = lax.dynamic_slice_in_dim(twice, (4 - x) % 4, 4, 0)
    rows = jnp.where(c == 0, rows, rows[:, ::-1])
    return rows.reshape(128, -1)


def rows_dot(a, b):
    return lax.dot_general(a, b, (((1,), (1,)), ((), ())), preferred_element_type=F32)


def after(value, *tokens):
    return lax.optimization_barrier((value,) + tokens)[0]


LAG = {"y1": 99, "y3": 99, "z": 2}


class Lanes:
    def __init__(self):
        self.done = {"y1": [], "y3": [], "z": []}

    def send(self, lane, value, to):
        past = self.done[lane]
        lag = LAG[lane]
        if len(past) >= lag:
            value = after(value, past[-lag])
        got = dp_move(value, to)
        past.append(got)
        return got


class Gather:
    def __init__(self, lanes, block, first):
        self.lanes, self.block, self.first = lanes, block, first

    def one(self):
        self.near = self.lanes.send("y%d" % self.first, self.block, swap(self.first))

    def two(self):
        other = 4 - self.first
        both = jnp.concatenate([self.block, self.near], 0)
        got = self.got = self.lanes.send("y%d" % other, both, swap(other))

    def rows(self, *tokens):
        other = 4 - self.first
        got = after(self.got, *tokens) if tokens else self.got
        n = self.block.shape[0]
        found = {0: self.block, self.first: self.near, other: got[:n], 2: got[n:]}
        return jnp.concatenate([found[r] for r in range(4)], 0)


class Scatter:
    def __init__(self, lanes, parts, first):
        self.lanes, self.parts, self.first = lanes, parts, first

    def one(self):
        first, other = self.first, 4 - self.first
        both = jnp.concatenate([self.parts[first], self.parts[2]], 0)
        got = self.lanes.send("y%d" % first, both, swap(first))
        n = self.parts[0].shape[0]
        self.mine = self.parts[0].astype(F32) + got[:n].astype(F32)
        self.give = (self.parts[other].astype(F32) + got[n:].astype(F32)).astype(BF16)

    def two(self):
        other = 4 - self.first
        got = self.lanes.send("y%d" % other, self.give, swap(other))
        self.total = self.mine + got.astype(F32)


def pair(a, b):
    a.one()
    b.one()
    a.two()
    b.two()


def shares(part, first=(), second=()):
    give = part[:, 1].astype(BF16)
    got = tensor_move(after(give, *first) if first else give, 0, 1)
    pair = part[:, 0] + got.astype(F32)
    if second:
        pair = after(pair, *second)
    mine = pair[:, 0]
    for moved in [tensor_move(pair[:, dx].astype(BF16), dx, 0) for dx in (1, 3, 2)]:
        mine = mine + moved.astype(F32)
    return mine.astype(BF16)


def swap_sections(mine):
    return lax.ppermute(mine, "section", [(0, 1), (1, 0)])


def spread_x(arrived):
    chunks = [arrived] + [tensor_move(arrived, -dx, 0) for dx in (1, 2, 3)]
    return jnp.stack(chunks, 1)


def spread_core(near):
    other = tensor_move(near, 0, 1)
    return jnp.stack([near, other], 1).reshape(near.shape[0] * 128, -1), other


class Halves:
    def __init__(self, kind, lanes, blocks):
        self.kind = kind
        if kind is Gather:
            n = blocks.shape[0] // 2
            self.parts = [Gather(lanes, blocks[:n], 1), Gather(lanes, blocks[n:], 3)]
        else:
            n = blocks[0].shape[0] // 2
            self.parts = [Scatter(lanes, [b[:n] for b in blocks], 1), Scatter(lanes, [b[n:] for b in blocks], 3)]

    def rows(self):
        return self.all

    def run(self):
        self.parts[0].one()
        self.parts[1].one()
        self.two()

    def two(self):
        self.parts[0].two()
        self.parts[1].two()
        if self.kind is Gather:
            low, high = [p.rows().reshape(4, 64, -1) for p in self.parts]
            self.all = jnp.concatenate([low, high], 1).reshape(512, -1)
        else:
            self.total = jnp.concatenate([p.total for p in self.parts], 0)


def fence(*values):
    return lax.optimization_barrier(values)


def cat(*blocks):
    return jnp.concatenate(blocks, 0)


def body(value_grad, value_weight, context, out_weight):
    w1 = value_weight[0]
    w2 = out_weight[0]
    lanes = Lanes()

    def partial(rows):
        return rows_dot(rows, w1).reshape(4, 2, 4, 16, 768)

    def matmul3(got):
        cpart = rows_dot(got, w2).astype(BF16).reshape(2, 4, 128, 1536)
        return [[cpart[i, b] for b in range(4)] for i in range(2)]

    def over_core(part):
        got = tensor_move(part[:, 1].astype(BF16), 0, 1)
        return part[:, 0] + got.astype(F32)

    vg0 = roll_in(value_grad[0])
    v0 = Halves(Gather, lanes, vg0)
    vg1 = lanes.send("z", vg0, down)
    vg2 = lanes.send("z", vg1, down)
    vg3 = lanes.send("z", vg0, up)
    v0.run()
    v1 = Halves(Gather, lanes, vg1)
    v1.run()
    part0 = partial(v0.rows())
    rows1, part0, vg2, vg3, cin = fence(v1.rows(), part0, vg2, vg3, context[0])

    near2 = dp_move(vg2, swap(1))
    near3 = dp_move(vg3, swap(3))
    pair_a = over_core(cat(part0, partial(rows1)))
    c0 = roll_in(cin)
    c1 = dp_move(c0, down)
    near2, near3, pair_a, c0, c1 = fence(near2, near3, pair_a, c0, c1)
    far2 = dp_move(cat(vg2, near2), swap(3))
    far3 = dp_move(cat(vg3, near3), swap(1))
    c2 = dp_move(c1, down)
    mine, moved = pair_a[:, 0], [tensor_move(pair_a[:, dx].astype(BF16), dx, 0) for dx in (1, 3, 2)]
    near2, far2, near3, far3, mine, *moved, c0, c1, c2 = fence(near2, far2, near3, far3, mine, *moved, c0, c1, c2)
    shares_a = (mine + moved[0].astype(F32) + moved[1].astype(F32) + moved[2].astype(F32)).astype(BF16)
    rows = cat(vg2, near2, far2[128:], far2[:128], vg3, far3[:128], far3[128:], near3)
    part_b = rows_dot(rows, w1).reshape(8, 2, 4, 16, 768)

    near0 = dp_move(c0, swap(1))
    near1 = dp_move(c1, swap(3))
    arrived_a = swap_sections(shares_a)
    pair_b = over_core(part_b)
    far0 = dp_move(cat(c0, near0), swap(3))
    far1 = dp_move(cat(c1, near1), swap(1))
    near_a = spread_x(arrived_a)
    mine = pair_b[:, 0]
    moved = [tensor_move(pair_b[:, dx].astype(BF16), dx, 0) for dx in (1, 3, 2)]
    near0, near1, far0, far1, c0, c1, c2, mine, near_a, *moved = fence(near0, near1, far0, far1, c0, c1, c2, mine, near_a, *moved)
    shares_b = (mine + moved[0].astype(F32) + moved[1].astype(F32) + moved[2].astype(F32)).astype(BF16)
    ctx = {0: cat(c0, near0, far0[128:], far0[:128]), 1: cat(c1, far1[:128], far1[128:], near1)}

    near2 = dp_move(c2[:64], swap(1))
    near3 = dp_move(c2[64:], swap(3))
    arrived_b = swap_sections(shares_b)
    rows_a, _ = spread_core(near_a)
    blocks_a = matmul3(rows_a)
    near2, near3, arrived_b, rows_a, ctx[0], *flat = fence(near2, near3, arrived_b, rows_a, ctx[0], *blocks_a[0], *blocks_a[1])
    blocks_a = [flat[:4], flat[4:]]

    sa = [Scatter(lanes, blocks_a[i], (1, 3)[i]) for i in range(2)]
    lanes.done = {"y1": [], "y3": [], "z": []}
    sa[0].one()
    sa[1].one()
    rows_b, _ = spread_core(spread_x(arrived_b))
    low = dp_move(ctx[0][:128], up)
    mine0, give0, mine1, give1, near2, near3, low, high, rows_b = fence(
        sa[0].mine, sa[0].give, sa[1].mine, sa[1].give, near2, near3, low, ctx[0][128:], rows_b
    )
    sa[0].mine, sa[0].give, sa[1].mine, sa[1].give = mine0, give0, mine1, give1
    blocks_b = matmul3(rows_b)
    high = dp_move(high, up)

    lanes.done = {"y1": [], "y3": [], "z": []}
    sb = [Scatter(lanes, blocks_b[i], (1, 3)[i]) for i in range(2)]
    sb[0].one()
    sb[1].one()
    lanes.done = {"y1": [], "y3": [], "z": []}
    sa[0].two()
    sa[1].two()
    total0, total1, mine2, give2, mine3, give3, near2, near3, low, high, rows_a, rows_b = fence(
        sa[0].total, sa[1].total, sb[0].mine, sb[0].give, sb[1].mine, sb[1].give, near2, near3, low, high, rows_a, rows_b
    )
    ctx[3] = cat(low, high)
    sb[0].mine, sb[0].give, sb[1].mine, sb[1].give = mine2, give2, mine3, give3

    lanes.done = {"y1": [], "y3": [], "z": []}
    sb[0].two()
    sb[1].two()
    z1 = dp_move(total1.astype(BF16), up)
    far2 = dp_move(cat(c2[:64], near2), swap(3))
    far3 = dp_move(cat(c2[64:], near3), swap(1))
    ctx[2] = cat(c2, near2, far3[:64], far2[64:], far3[64:], far2[:64], near3)
    z2 = dp_move(sb[0].total.astype(BF16), across)
    z3 = dp_move(sb[1].total.astype(BF16), down)
    result = total0 + z1.astype(F32) + z2.astype(F32) + z3.astype(F32)

    def grad(k, rows):
        return lax.dot_general(ctx[k], rows, (((0,), (0,)), ((), ())), preferred_element_type=F32)

    out_grad = grad(0, rows_a[:512]) + grad(1, rows_a[512:]) + grad(2, rows_b[:512]) + grad(3, rows_b[512:])
    return out_grad.astype(BF16)[None], roll_out(result.astype(BF16))[None]


def solution(mesh):
    in_specs = (
        P("section", "dp", "tensor"),
        P("section", "dp", "tensor"),
        P("section", "dp", "tensor"),
        P("section", "tensor", "dp"),
    )
    out_specs = (P("section", "tensor", "dp"), P("section", "dp", "tensor"))
    return jax.shard_map(body, mesh=mesh, in_specs=in_specs, out_specs=out_specs, check_vma=False)
```

```python
import jax
import jax.numpy as jnp
from jax import lax
from jax.sharding import PartitionSpec as P

F32 = jnp.float32
BF16 = jnp.bfloat16


def dp_move(shard, to):
    pairs = []
    for z in range(4):
        for y in range(4):
            z2, y2 = to(z, y)
            pairs.append((z * 4 + y, z2 % 4 * 4 + y2 % 4))
    return lax.ppermute(shard, "dp", pairs)


def up(z, y):
    return z + 1, y


def down(z, y):
    return z - 1, y


def across(z, y):
    return z + 2, y


def swap(r):
    return lambda z, y: (z, y ^ r)


def tensor_move(shard, dx, dc):
    pairs = [
        (x * 2 + c, (x + dx) % 4 * 2 + (c + dc) % 2) for x in range(4) for c in range(2)
    ]
    return lax.ppermute(shard, "tensor", pairs)


def roll_in(block):
    t = lax.axis_index("tensor")
    x, c = t // 2, t % 2
    rows = block.reshape(4, 2, 16, -1)
    rows = jnp.where(c == 0, rows, rows[:, ::-1])
    twice = jnp.concatenate([rows, rows], 0)
    rows = lax.dynamic_slice_in_dim(twice, x, 4, 0)
    return rows.transpose(1, 0, 2, 3).reshape(128, -1)


def roll_out(block):
    t = lax.axis_index("tensor")
    x, c = t // 2, t % 2
    rows = block.reshape(2, 4, 16, -1).transpose(1, 0, 2, 3)
    twice = jnp.concatenate([rows, rows], 0)
    rows = lax.dynamic_slice_in_dim(twice, (4 - x) % 4, 4, 0)
    rows = jnp.where(c == 0, rows, rows[:, ::-1])
    return rows.reshape(128, -1)


def rows_dot(a, b):
    return lax.dot_general(a, b, (((1,), (1,)), ((), ())), preferred_element_type=F32)


def after(value, *tokens):
    return lax.optimization_barrier((value,) + tokens)[0]


LAG = {"y1": 99, "y3": 99, "z": 99}


class Lanes:
    def __init__(self):
        self.done = {"y1": [], "y3": [], "z": []}

    def send(self, lane, value, to):
        past = self.done[lane]
        lag = LAG[lane]
        if len(past) >= lag:
            value = after(value, past[-lag])
        got = dp_move(value, to)
        past.append(got)
        return got


class Gather:
    def __init__(self, lanes, block, first):
        self.lanes, self.block, self.first = lanes, block, first

    def one(self):
        self.near = self.lanes.send("y%d" % self.first, self.block, swap(self.first))

    def two(self):
        other = 4 - self.first
        both = jnp.concatenate([self.block, self.near], 0)
        got = self.got = self.lanes.send("y%d" % other, both, swap(other))

    def rows(self, *tokens):
        other = 4 - self.first
        got = after(self.got, *tokens) if tokens else self.got
        n = self.block.shape[0]
        found = {0: self.block, self.first: self.near, other: got[:n], 2: got[n:]}
        return jnp.concatenate([found[r] for r in range(4)], 0)


class Scatter:
    def __init__(self, lanes, parts, first):
        self.lanes, self.parts, self.first = lanes, parts, first

    def one(self):
        first, other = self.first, 4 - self.first
        both = jnp.concatenate([self.parts[first], self.parts[2]], 0)
        got = self.lanes.send("y%d" % first, both, swap(first))
        n = self.parts[0].shape[0]
        self.mine = self.parts[0].astype(F32) + got[:n].astype(F32)
        self.give = (self.parts[other].astype(F32) + got[n:].astype(F32)).astype(BF16)

    def two(self):
        other = 4 - self.first
        got = self.lanes.send("y%d" % other, self.give, swap(other))
        self.total = self.mine + got.astype(F32)


def pair(a, b):
    a.one()
    b.one()
    a.two()
    b.two()


def shares(part, first=(), second=()):
    give = part[:, 1].astype(BF16)
    got = tensor_move(after(give, *first) if first else give, 0, 1)
    pair = part[:, 0] + got.astype(F32)
    if second:
        pair = after(pair, *second)
    mine = pair[:, 0]
    for moved in [tensor_move(pair[:, dx].astype(BF16), dx, 0) for dx in (1, 3, 2)]:
        mine = mine + moved.astype(F32)
    return mine.astype(BF16)


def swap_sections(mine):
    return lax.ppermute(mine, "section", [(0, 1), (1, 0)])


def spread_x(arrived):
    chunks = [arrived] + [tensor_move(arrived, -dx, 0) for dx in (1, 2, 3)]
    return jnp.stack(chunks, 1)


def spread_core(near):
    other = tensor_move(near, 0, 1)
    return jnp.stack([near, other], 1).reshape(near.shape[0] * 128, -1), other


class Halves:
    def __init__(self, kind, lanes, blocks):
        self.kind = kind
        if kind is Gather:
            n = blocks.shape[0] // 2
            self.parts = [Gather(lanes, blocks[:n], 1), Gather(lanes, blocks[n:], 3)]
        else:
            n = blocks[0].shape[0] // 2
            self.parts = [Scatter(lanes, [b[:n] for b in blocks], 1), Scatter(lanes, [b[n:] for b in blocks], 3)]

    def rows(self):
        return self.all

    def run(self):
        self.parts[0].one()
        self.parts[1].one()
        self.two()

    def two(self):
        self.parts[0].two()
        self.parts[1].two()
        if self.kind is Gather:
            low, high = [p.rows().reshape(4, 64, -1) for p in self.parts]
            self.all = jnp.concatenate([low, high], 1).reshape(512, -1)
        else:
            self.total = jnp.concatenate([p.total for p in self.parts], 0)


def fence(*values):
    return lax.optimization_barrier(values)


def cat(*blocks):
    return jnp.concatenate(blocks, 0)


def body(value_grad, value_weight, context, out_weight):
    w1 = value_weight[0]
    w2 = out_weight[0]
    lanes = Lanes()

    def partial(rows):
        return rows_dot(rows, w1).reshape(4, 2, 4, 16, 768)

    def matmul3(got):
        cpart = rows_dot(got, w2).astype(BF16).reshape(2, 4, 128, 1536)
        return [[cpart[i, b] for b in range(4)] for i in range(2)]

    def over_core(part):
        got = tensor_move(part[:, 1].astype(BF16), 0, 1)
        return part[:, 0] + got.astype(F32)

    vg0 = roll_in(value_grad[0])
    v0 = Halves(Gather, lanes, vg0)
    vg1 = lanes.send("z", vg0, down)
    vg2 = lanes.send("z", vg1, down)
    vg3 = lanes.send("z", vg0, up)
    v0.run()
    v1 = Halves(Gather, lanes, vg1)
    v1.run()
    part0 = partial(v0.rows())
    rows1, part0, vg2, vg3, cin = fence(v1.rows(), part0, vg2, vg3, context[0])

    near2 = dp_move(vg2, swap(1))
    near3 = dp_move(vg3, swap(3))
    pair_a = over_core(cat(part0, partial(rows1)))
    c0 = roll_in(cin)
    c1 = dp_move(c0, down)
    c1 = after(c1, near2, near3)
    far2 = dp_move(cat(vg2, near2), swap(3))
    far3 = dp_move(cat(vg3, near3), swap(1))
    c2 = dp_move(c1, down)
    mine, moved = pair_a[:, 0], [tensor_move(pair_a[:, dx].astype(BF16), dx, 0) for dx in (1, 3, 2)]
    near2, far2, near3, far3, mine, *moved, c0, c1, c2 = fence(near2, far2, near3, far3, mine, *moved, c0, c1, c2)
    shares_a = (mine + moved[0].astype(F32) + moved[1].astype(F32) + moved[2].astype(F32)).astype(BF16)
    rows = cat(vg2, near2, far2[128:], far2[:128], vg3, far3[:128], far3[128:], near3)
    part_b = rows_dot(rows, w1).reshape(8, 2, 4, 16, 768)

    near0 = dp_move(c0, swap(1))
    near1 = dp_move(c1, swap(3))
    arrived_a = swap_sections(shares_a)
    pair_b = over_core(part_b)
    far0 = dp_move(cat(c0, near0), swap(3))
    far1 = dp_move(cat(c1, near1), swap(1))
    near_a = spread_x(arrived_a)
    mine = pair_b[:, 0]
    moved = [tensor_move(pair_b[:, dx].astype(BF16), dx, 0) for dx in (1, 3, 2)]
    near0, near1, far0, far1, c0, c1, c2, mine, near_a, *moved = fence(near0, near1, far0, far1, c0, c1, c2, mine, near_a, *moved)
    shares_b = (mine + moved[0].astype(F32) + moved[1].astype(F32) + moved[2].astype(F32)).astype(BF16)
    ctx = {0: cat(c0, near0, far0[128:], far0[:128]), 1: cat(c1, far1[:128], far1[128:], near1)}

    near2 = dp_move(c2[:64], swap(1))
    near3 = dp_move(c2[64:], swap(3))
    arrived_b = swap_sections(shares_b)
    rows_a, _ = spread_core(near_a)
    blocks_a = matmul3(rows_a)
    near2, near3, arrived_b, rows_a, ctx[0], *flat = fence(near2, near3, arrived_b, rows_a, ctx[0], *blocks_a[0], *blocks_a[1])
    blocks_a = [flat[:4], flat[4:]]

    sa = [Scatter(lanes, blocks_a[i], (1, 3)[i]) for i in range(2)]
    lanes.done = {"y1": [], "y3": [], "z": []}
    sa[0].one()
    sa[1].one()
    rows_b, _ = spread_core(spread_x(arrived_b))
    low = dp_move(ctx[0][:128], up)
    mine0, give0, mine1, give1, near2, near3, low, high, rows_b = fence(
        sa[0].mine, sa[0].give, sa[1].mine, sa[1].give, near2, near3, low, ctx[0][128:], rows_b
    )
    sa[0].mine, sa[0].give, sa[1].mine, sa[1].give = mine0, give0, mine1, give1
    blocks_b = matmul3(rows_b)
    high = dp_move(high, up)

    lanes.done = {"y1": [], "y3": [], "z": []}
    sb = [Scatter(lanes, blocks_b[i], (1, 3)[i]) for i in range(2)]
    sb[0].one()
    sb[1].one()
    lanes.done = {"y1": [], "y3": [], "z": []}
    sa[0].two()
    sa[1].two()
    total0, total1, mine2, give2, mine3, give3, near2, near3, low, high, rows_a, rows_b = fence(
        sa[0].total, sa[1].total, sb[0].mine, sb[0].give, sb[1].mine, sb[1].give, near2, near3, low, high, rows_a, rows_b
    )
    ctx[3] = cat(low, high)
    sb[0].mine, sb[0].give, sb[1].mine, sb[1].give = mine2, give2, mine3, give3

    lanes.done = {"y1": [], "y3": [], "z": []}
    sb[0].two()
    sb[1].two()
    z1 = dp_move(total1.astype(BF16), up)
    far2 = dp_move(cat(c2[:64], near2), swap(3))
    far3 = dp_move(cat(c2[64:], near3), swap(1))
    ctx[2] = cat(c2, near2, far3[:64], far2[64:], far3[64:], far2[:64], near3)
    z2 = dp_move(sb[0].total.astype(BF16), across)
    z3 = dp_move(sb[1].total.astype(BF16), down)
    result = total0 + z1.astype(F32) + z2.astype(F32) + z3.astype(F32)

    def grad(k, rows):
        return lax.dot_general(ctx[k], rows, (((0,), (0,)), ((), ())), preferred_element_type=F32)

    out_grad = grad(0, rows_a[:512]) + grad(1, rows_a[512:]) + grad(2, rows_b[:512]) + grad(3, rows_b[512:])
    return out_grad.astype(BF16)[None], roll_out(result.astype(BF16))[None]


def solution(mesh):
    in_specs = (
        P("section", "dp", "tensor"),
        P("section", "dp", "tensor"),
        P("section", "dp", "tensor"),
        P("section", "tensor", "dp"),
    )
    out_specs = (P("section", "tensor", "dp"), P("section", "dp", "tensor"))
    return jax.shard_map(body, mesh=mesh, in_specs=in_specs, out_specs=out_specs, check_vma=False)
```
